32 devices in a mesh: tm: 4 (over y, core), panel: 8 (over z, x).
Axes of the slice: x: 2, y: 2, z: 4, core: 2. Of those that a mesh axis runs over, the one named last changes fastest.
Arguments:
- pressure: float32 [4096, 16384], P('tm', 'panel'), may hold values from -6 to 6
- freq_bins: int32 [64], replicated, may hold values from 1 to 2047
- stencil_ids: int32 [4096, 16], P('panel'), may hold values from 0 to 2047
- spline_weights: float32 [4096, 16], P('panel'), may hold values from -2 to 2
- mode_forces: float32 [32, 4096], P(None, 'panel'), may hold values from -0.09375 to 0.09375
- mode_washes: float32 [32, 4096], P(None, 'panel'), may hold values from -6 to 6
Outputs:
- grams: float32 [2, 64, 32, 32], replicated
The draws below stay inside these ranges and needn't reach their ends.
Inputs may be any that keep to these rules, and one draw needn't show every extreme that they name: `freq_bins`: frequency bins of the excitation lines, possibly repeated. `stencil_ids`: indices within the point group of the panel, group p // 512.
All inputs are finite; a program needn't handle non-finite values.
Results may differ from the reference program's by a relative error of at most 0.000073.
Values sent between devices are 32-bit elements; how exact they have to be, the bound alone decides.
A program may use at most 64 MiB of HBM per device.

```python
import math
import jax
import jax.numpy as jnp
from jax import lax

NT = 4096
NF = 64
M = 32
K = 16
PTS_PAN = 2048
PAN_DEV = 512
NPTS = 16384
PANELS = 4096


def place_ends(values, own_key, low, largest):
    spot = [jax.random.randint(jax.random.fold_in(own_key, axis), (), 0, length) for axis, length in enumerate(values.shape)]
    widest = values.shape.index(max(values.shape))
    neighbour = spot[:widest] + [(spot[widest] + 1) % values.shape[widest]] + spot[widest + 1:]
    return values.at[tuple(spot)].set(low).at[tuple(neighbour)].set(largest)


def with_spikes(array, own_key, source, target, blocks, factor):
    def block_of(axis_at):
        return (jnp.arange(array.shape[axis_at]) // (array.shape[axis_at] // blocks)).reshape((-1,) + (1,) * (array.ndim - 1 - axis_at))

    first = jax.random.permutation(own_key, blocks)[block_of(target)]
    other_side = (block_of(target) + blocks // 2) % blocks
    return jnp.where((block_of(source) == first) | (block_of(source) == other_side), factor * array, array)


def levels(stream_key, shape, split, smallest, largest):
    def one(position, parts):
        heights = jax.random.uniform(jax.random.fold_in(jax.random.fold_in(stream_key, 6), position), (parts,), jnp.float32, smallest / len(split), largest / len(split))
        return jnp.repeat(jnp.exp(heights), shape[position] // parts).reshape((-1,) + (1,) * (len(shape) - position - 1))

    gain = one(*split[0])
    for cut in split[1:]:
        gain = gain * one(*cut)
    return gain


def scatter_about(own_key, dims, spread, reach, cuts=(), held_as=jnp.bfloat16):
    drawn = spread * jax.random.normal(own_key, dims, jnp.float32)
    if cuts:
        drawn = drawn * levels(own_key, dims, cuts, -0.22, 0.18)
    return jnp.clip(drawn, -reach, reach).astype(held_as)


def gaussian_with(rng, extent, width, limit, split, heavy, kind=jnp.bfloat16):
    entries = width * jax.random.normal(rng, extent, jnp.float32)
    if split:
        entries = entries * levels(rng, extent, split, -0.22, 0.18)
    return jnp.clip(with_spikes(entries, jax.random.fold_in(rng, 3), *heavy), -limit, limit).astype(kind)


def setup_inputs(seed: int = 0) -> dict:
    seeds = jax.random.split(jax.random.key(seed), 7)
    return {
        "pressure": gaussian_with(seeds[0], (NT, NPTS), 1.0, 6.0, ((0, 4), (1, 8)), (0, 1, 8, 2.0), jnp.float32),
        "freq_bins": place_ends(jax.random.randint(seeds[1], (NF,), 1, NT // 2), jax.random.fold_in(seeds[1], 1), 1, (NT // 2) - 1).astype(jnp.int32),
        "stencil_ids": place_ends(jax.random.randint(seeds[2], (PANELS, K), 0, PTS_PAN), jax.random.fold_in(seeds[2], 1), 0, PTS_PAN - 1).astype(jnp.int32),
        "spline_weights": scatter_about(seeds[3], (PANELS, K), 0.35, 2.0, ((0, 8),), jnp.float32),
        "mode_forces": scatter_about(seeds[4], (M, PANELS), PANELS ** -0.5, 0.09375, ((1, 8),), jnp.float32),
        "mode_washes": scatter_about(seeds[5], (M, PANELS), 1.0, 6.0, ((1, 8),), jnp.float32),
    }


def dft_table(freq_bins, first, length, total):
    times = first + jnp.arange(length, dtype=jnp.int32)
    phase = freq_bins[:, None] * times[None, :] % total
    angle = 2.0 * math.pi / total * phase.astype(jnp.float32)
    scale_value = 1.0 / math.sqrt(total)
    return jnp.concatenate([jnp.cos(angle), -jnp.sin(angle)], axis=0) * scale_value

def reference(pressure, freq_bins, stencil_ids, spline_weights, mode_forces, mode_washes):
    table = dft_table(freq_bins, 0, NT, NT)
    spectra = jnp.dot(table, pressure, precision=lax.Precision.HIGHEST, preferred_element_type=jnp.float32)
    groups = (jnp.arange(PANELS, dtype=jnp.int32) // PAN_DEV).astype(jnp.int32)
    columns = (groups[:, None] * PTS_PAN + stencil_ids).astype(jnp.int32)
    picked = spectra[:, columns]
    panel_spectra = lax.optimization_barrier(jnp.sum(picked * spline_weights[None, :, :], axis=-1))
    weighted = panel_spectra[:, None, :] * mode_forces[None, :, :]
    grams = lax.dot_general(weighted, mode_washes, (((2,), (1,)), ((), ())), precision=lax.Precision.HIGHEST, preferred_element_type=jnp.float32)
    return grams.reshape(2, NF, M, M)
```

```python
import functools
import math

import jax
import jax.numpy as jnp
from jax import lax
from jax.experimental import pallas as pl
from jax.experimental.pallas import tpu as pltpu
from jax.sharding import PartitionSpec as P

F32 = jnp.float32
BF16 = jnp.bfloat16
LANES = 128
CHUNK = 256
MESH = pl.DeviceIdType.MESH


def split_pair(value):
    high = value.astype(BF16)
    return high, (value - high.astype(F32)).astype(BF16)


def dot_rows(left, right):
    return lax.dot_general(left, right, (((1,), (0,)), ((), ())), preferred_element_type=F32)


def dot_lanes(left, right):
    return lax.dot_general(left, right, (((1,), (1,)), ((), ())), preferred_element_type=F32)


def fill_table(freq_ref, table_ref, first, total):
    freqs = freq_ref.shape[1]
    steps = table_ref.shape[1]
    quarter = total // 4
    spread = jnp.broadcast_to(freq_ref[...].astype(F32), (freqs, freqs))
    on_diagonal = lax.broadcasted_iota(jnp.int32, (freqs, freqs), 0) == lax.broadcasted_iota(
        jnp.int32, (freqs, freqs), 1
    )
    column = jnp.sum(jnp.where(on_diagonal, spread, 0.0), axis=1, keepdims=True).astype(jnp.int32)
    scale = 1.0 / math.sqrt(total)
    width = 2 * LANES

    def fill(block, carry):
        at = pl.multiple_of(block * width, width)
        times = lax.broadcasted_iota(jnp.int32, (freqs, width), 1) + (first + at)
        phase = (column * times) & (total - 1)
        turn = (phase + quarter // 2) >> (quarter.bit_length() - 1)
        x = (phase - turn * quarter).astype(F32) * (2.0 * math.pi / total)
        z = x * x
        sine = x + x * z * (-1.6666654611e-1 + z * (8.3321608736e-3 + z * -1.9515295891e-4))
        cosine = 1.0 - 0.5 * z + z * z * (
            4.166664568298827e-2 + z * (-1.388731625493765e-3 + z * 2.443315711809948e-5)
        )
        odd = (turn & 1) == 1
        cos_raw = jnp.where(odd, sine, cosine)
        sin_raw = jnp.where(odd, cosine, sine)
        cos_sign = jnp.where(((turn + 1) & 2) == 2, -scale, scale)
        sin_sign = jnp.where((turn & 2) == 2, scale, -scale)
        cos_high, cos_low = split_pair(cos_raw * cos_sign)
        sin_high, sin_low = split_pair(sin_raw * sin_sign)
        for place, part in enumerate((cos_high, sin_high, cos_low, sin_low)):
            table_ref[place * freqs:(place + 1) * freqs, pl.ds(at, width)] = part
        return carry

    lax.fori_loop(0, steps // width, fill, 0)


def fill_stencils(ids_ref, weights_ref, ids_rows, high_rows, low_rows):
    ids = ids_ref[...]
    weights = weights_ref[...]
    count = ids.shape[0]
    merged = weights
    for shift in range(1, count):
        same = pltpu.roll(ids, shift, 0) == ids
        merged = merged + jnp.where(same, pltpu.roll(weights, shift, 0), 0.0)
    high, low = split_pair(merged)
    high = high.astype(F32)
    low = low.astype(F32)
    for k in range(count):
        rows = slice(16 * k, 16 * k + 16)
        full = (16, ids.shape[1])
        ids_rows[rows, :] = jnp.broadcast_to(ids[k:k + 1, :], full).astype(jnp.int16)
        high_rows[rows, :] = jnp.broadcast_to(high[k:k + 1, :], full).astype(BF16)
        low_rows[rows, :] = jnp.broadcast_to(low[k:k + 1, :], full).astype(BF16)


def fill_basis(base, points, ids_rows, high_rows, low_rows, basis_high, basis_low):
    count = ids_rows.shape[0] // 16
    group = 8
    for half in range(points // (16 * group)):
        rows_at = [half * 16 * group + 16 * g for g in range(group)]
        wanted = [
            (lax.broadcasted_iota(jnp.int32, (16, LANES), 0) + (base + at)).astype(jnp.int16) for at in rows_at
        ]
        for tile in range(ids_rows.shape[1] // LANES):
            lanes = slice(tile * LANES, (tile + 1) * LANES)
            high = [jnp.zeros((16, LANES), BF16)] * group
            low = [jnp.zeros((16, LANES), BF16)] * group
            for k in range(count):
                rows = slice(16 * k, 16 * k + 16)
                ids_k = ids_rows[rows, lanes]
                high_k = high_rows[rows, lanes]
                low_k = low_rows[rows, lanes]
                for g in range(group):
                    hit = wanted[g] == ids_k
                    high[g] = jnp.where(hit, high_k, high[g])
                    low[g] = jnp.where(hit, low_k, low[g])
            for g in range(group):
                basis_high[rows_at[g]:rows_at[g] + 16, lanes] = high[g]
                basis_low[rows_at[g]:rows_at[g] + 16, lanes] = low[g]


def fill_products(forces_ref, washes_ref, high_ref, low_ref):
    modes = forces_ref.shape[0]

    def fill(m, carry):
        at = pl.multiple_of(m * modes, modes)
        high, low = split_pair(forces_ref[pl.ds(m, 1), :] * washes_ref[...])
        high_ref[pl.ds(at, modes), :] = high
        low_ref[pl.ds(at, modes), :] = low
        return carry

    lax.fori_loop(0, modes, fill, 0)


def kernel(
    tm_count, panel_count,
    pressure_ref, freq_in, ids_in, weights_in, forces_in, washes_in,
    out_ref,
    freq_ref, ids_ref, weights_ref, forces_ref, washes_ref,
    pressure_buf, table, ids_rows, high_rows, low_rows, basis_high, basis_low,
    partial, first_buf, product_high, product_low, local, second_buf, gathered,
    small_sem, load_sem, first_send, first_recv, second_send, second_recv,
    wide_send, wide_recv, core_send, core_recv, side_send, side_recv, last_send, last_recv,
):
    me_t = lax.axis_index("tm")
    me_p = lax.axis_index("panel")
    core = lax.rem(me_t, 2)
    side = me_t // 2
    sides = tm_count // 2

    def tm_at(rel):
        return 2 * lax.rem(side + rel // 2, sides) + lax.rem(core + rel % 2, 2)

    rels = range(1, tm_count)
    partner = tm_at(1)
    steps, points = pressure_ref.shape
    chunks = points // CHUNK
    cells = partial.shape[0]
    own_rows = cells // tm_count
    rows = local.shape[1]
    bands = own_rows // rows
    blocks = panel_count // bands

    def load(j):
        return pltpu.make_async_copy(
            pressure_ref.at[:, pl.ds(pl.multiple_of(j * CHUNK, CHUNK), CHUNK)], pressure_buf.at[j], load_sem.at[j]
        )

    small = [
        pltpu.make_async_copy(source, target, small_sem.at[place])
        for place, (source, target) in enumerate((
            (freq_in, freq_ref), (ids_in, ids_ref), (weights_in, weights_ref),
            (forces_in, forces_ref), (washes_in, washes_ref),
        ))
    ]
    for copy in small:
        copy.start()
    for j in range(chunks):
        load(j).start()

    barrier = pltpu.get_barrier_semaphore()
    for rel in rels:
        pl.semaphore_signal(barrier, inc=1, device_id=(tm_at(rel), me_p), device_id_type=MESH)
    for d in range(1, panel_count):
        pl.semaphore_signal(
            barrier, inc=1, device_id=(me_t, lax.rem(me_p + d, panel_count)), device_id_type=MESH
        )

    small[0].wait()
    fill_table(freq_ref, table, me_t * steps, steps * tm_count)
    small[1].wait()
    small[2].wait()
    fill_stencils(ids_ref, weights_ref, ids_rows, high_rows, low_rows)
    partial[...] = jnp.zeros_like(partial)

    def chunk_step(j, carry):
        load(j).wait()
        block_high, block_low = split_pair(pressure_buf[j])
        wide = dot_rows(table[...], block_high)
        spectra = wide[:cells] + wide[cells:] + dot_rows(table[:cells, :], block_low)
        fill_basis(j * CHUNK, CHUNK, ids_rows, high_rows, low_rows, basis_high, basis_low)
        spectra_high, spectra_low = split_pair(spectra)
        partial[...] += (
            dot_rows(spectra_high, basis_high[...])
            + dot_rows(spectra_low, basis_high[...])
            + dot_rows(spectra_high, basis_low[...])
        )
        return carry

    lax.fori_loop(0, chunks, chunk_step, 0)

    pl.semaphore_wait(barrier, tm_count + panel_count - 2)

    first = {}
    for rel in reversed(rels):
        first[rel] = pltpu.make_async_remote_copy(
            src_ref=partial.at[pl.ds(pl.multiple_of(tm_at(rel) * own_rows, own_rows), own_rows)],
            dst_ref=first_buf.at[rel - 1],
            send_sem=first_send.at[rel - 1],
            recv_sem=first_recv.at[rel - 1],
            device_id=(tm_at(rel), me_p),
            device_id_type=MESH,
        )
        first[rel].start()
    small[3].wait()
    small[4].wait()
    fill_products(forces_ref, washes_ref, product_high, product_low)
    owned = partial[pl.ds(pl.multiple_of(me_t * own_rows, own_rows), own_rows), :]
    for rel in rels:
        first[rel].wait_recv()
        owned = owned + first_buf[rel - 1]
    owned_high, owned_low = split_pair(owned)
    for pair in range(blocks // 2):
        span = slice(pair * 2 * LANES, (pair + 1) * 2 * LANES)
        grams = (
            dot_lanes(owned_high, product_high[span, :])
            + dot_lanes(owned_low, product_high[span, :])
            + dot_lanes(owned_high, product_low[span, :])
        )
        for part in range(2):
            for band in range(bands):
                local[band * blocks + 2 * pair + part] = grams[
                    band * rows:(band + 1) * rows, part * LANES:(part + 1) * LANES
                ]

    second = []
    for d in range(1, panel_count):
        target = lax.rem(me_p + d, panel_count)
        copy = pltpu.make_async_remote_copy(
            src_ref=local.at[target],
            dst_ref=second_buf.at[d - 1],
            send_sem=second_send.at[d - 1],
            recv_sem=second_recv.at[d - 1],
            device_id=(me_t, target),
            device_id_type=MESH,
        )
        copy.start()
        second.append(copy)
    total = local[me_p]
    for d in range(1, panel_count):
        second[d - 1].wait_recv()
        total = total + second_buf[d - 1]
    gathered[me_t, me_p] = total

    def share(p, t, sends, recvs, index, device):
        place = gathered.at[t, p]
        copy = pltpu.make_async_remote_copy(
            src_ref=place,
            dst_ref=place,
            send_sem=sends.at[index],
            recv_sem=recvs.at[index],
            device_id=device,
            device_id_type=MESH,
        )
        return copy

    wide, to_core, to_side, last = [], [], [], []
    for d in range(1, panel_count):
        copy = share(me_p, me_t, wide_send, wide_recv, d - 1, (me_t, lax.rem(me_p + d, panel_count)))
        copy.start()
        wide.append(copy)
    for d in range(panel_count):
        origin = lax.rem(me_p + panel_count - d, panel_count)
        if d > 0:
            wide[d - 1].wait_recv()
        for hop in range(1, sides):
            copy = share(
                origin, me_t, side_send, side_recv, (hop - 1) * panel_count + d, (tm_at(2 * hop), me_p)
            )
            copy.start()
            to_side.append(copy)
        copy = share(origin, me_t, core_send, core_recv, d, (partner, me_p))
        copy.start()
        to_core.append(copy)
    for d in range(panel_count):
        origin = lax.rem(me_p + panel_count - d, panel_count)
        for hop in range(1, sides):
            to_side[d * (sides - 1) + hop - 1].wait_recv()
            copy = share(
                origin, tm_at(2 * (sides - hop)), last_send, last_recv, (hop - 1) * panel_count + d, (partner, me_p)
            )
            copy.start()
            last.append(copy)
    for copy in to_core + last:
        copy.wait_recv()

    def turn(block, carry):
        at = pl.multiple_of(block * LANES, LANES)
        for c in range(2):
            parts = [
                gathered[t, band * blocks + block]
                for t in range(c * sides, (c + 1) * sides)
                for band in range(bands)
            ]
            out_ref[c, pl.ds(at, LANES), :] = jnp.concatenate(parts, axis=0).T
        return carry

    lax.fori_loop(0, blocks, turn, 0)

    for copy in list(first.values()) + second + wide + to_core + to_side + last:
        copy.wait_send()


def body(pressure, freq_bins, stencil_ids, spline_weights, mode_forces, mode_washes):
    tm_count = lax.axis_size("tm")
    panel_count = lax.axis_size("panel")
    steps, points = pressure.shape
    freqs = freq_bins.shape[0]
    panels, stencil = stencil_ids.shape
    modes = mode_forces.shape[0]
    cells = 2 * freqs
    own_rows = cells // tm_count
    blocks = modes * modes // LANES
    rows = own_rows * blocks // panel_count
    chunks = points // CHUNK
    vmem = pl.BlockSpec(memory_space=pltpu.VMEM)
    peers = panel_count - 1
    far = (tm_count // 2 - 1) * panel_count
    dma = pltpu.SemaphoreType.DMA
    grams = pl.pallas_call(
        functools.partial(kernel, tm_count, panel_count),
        out_shape=jax.ShapeDtypeStruct((2, modes * modes, freqs), F32),
        in_specs=[pl.BlockSpec(memory_space=pl.ANY)] * 6,
        out_specs=vmem,
        scratch_shapes=[
            pltpu.VMEM((1, freqs), jnp.int32),
            pltpu.VMEM((stencil, panels), jnp.int32),
            pltpu.VMEM((stencil, panels), F32),
            pltpu.VMEM((modes, panels), F32),
            pltpu.VMEM((modes, panels), F32),
            pltpu.VMEM((chunks, steps, CHUNK), F32),
            pltpu.VMEM((2 * cells, steps), BF16),
            pltpu.VMEM((16 * stencil, panels), jnp.int16),
            pltpu.VMEM((16 * stencil, panels), BF16),
            pltpu.VMEM((16 * stencil, panels), BF16),
            pltpu.VMEM((CHUNK, panels), BF16),
            pltpu.VMEM((CHUNK, panels), BF16),
            pltpu.VMEM((cells, panels), F32),
            pltpu.VMEM((tm_count - 1, own_rows, panels), F32),
            pltpu.VMEM((modes * modes, panels), BF16),
            pltpu.VMEM((modes * modes, panels), BF16),
            pltpu.VMEM((panel_count, rows, LANES), F32),
            pltpu.VMEM((peers, rows, LANES), F32),
            pltpu.VMEM((tm_count, panel_count, rows, LANES), F32),
            dma((5,)),
            dma((chunks,)),
            dma((tm_count - 1,)), dma((tm_count - 1,)),
            dma((peers,)), dma((peers,)),
            dma((peers,)), dma((peers,)),
            dma((panel_count,)), dma((panel_count,)),
            dma((far,)), dma((far,)),
            dma((far,)), dma((far,)),
        ],
        compiler_params=pltpu.CompilerParams(
            collective_id=0, has_side_effects=True, vmem_limit_bytes=58 * 1024 * 1024
        ),
        cost_estimate=pl.CostEstimate(flops=4 * 10**9, bytes_accessed=10 * 2**20, transcendentals=0),
    )(
        pressure,
        freq_bins.reshape(1, freqs),
        stencil_ids.T,
        spline_weights.T,
        mode_forces,
        mode_washes,
    )
    return grams.reshape(2, modes, modes, freqs).transpose(0, 3, 1, 2)


def solution(mesh):
    placed = (
        P("tm", "panel"),
        P(),
        P("panel", None),
        P("panel", None),
        P(None, "panel"),
        P(None, "panel"),
    )
    return jax.shard_map(body, mesh=mesh, in_specs=placed, out_specs=P(), check_vma=False)
```

```python
import functools
import math

import jax
import jax.numpy as jnp
from jax import lax
from jax.experimental import pallas as pl
from jax.experimental.pallas import tpu as pltpu
from jax.sharding import PartitionSpec as P

F32 = jnp.float32
BF16 = jnp.bfloat16
LANES = 128
CHUNK = 512
MESH = pl.DeviceIdType.MESH


def split_pair(value):
    high = value.astype(BF16)
    return high, (value - high.astype(F32)).astype(BF16)


def dot_rows(left, right):
    return lax.dot_general(left, right, (((1,), (0,)), ((), ())), preferred_element_type=F32)


def dot_lanes(left, right):
    return lax.dot_general(left, right, (((1,), (1,)), ((), ())), preferred_element_type=F32)


def fill_table(freq_ref, table_ref, first, total):
    freqs = freq_ref.shape[1]
    steps = table_ref.shape[1]
    quarter = total // 4
    spread = jnp.broadcast_to(freq_ref[...].astype(F32), (freqs, freqs))
    on_diagonal = lax.broadcasted_iota(jnp.int32, (freqs, freqs), 0) == lax.broadcasted_iota(
        jnp.int32, (freqs, freqs), 1
    )
    column = jnp.sum(jnp.where(on_diagonal, spread, 0.0), axis=1, keepdims=True).astype(jnp.int32)
    scale = 1.0 / math.sqrt(total)
    width = 2 * LANES

    def fill(block, carry):
        at = pl.multiple_of(block * width, width)
        times = lax.broadcasted_iota(jnp.int32, (freqs, width), 1) + (first + at)
        phase = (column * times) & (total - 1)
        turn = (phase + quarter // 2) >> (quarter.bit_length() - 1)
        x = (phase - turn * quarter).astype(F32) * (2.0 * math.pi / total)
        z = x * x
        sine = x + x * z * (-1.6666654611e-1 + z * (8.3321608736e-3 + z * -1.9515295891e-4))
        cosine = 1.0 - 0.5 * z + z * z * (
            4.166664568298827e-2 + z * (-1.388731625493765e-3 + z * 2.443315711809948e-5)
        )
        odd = (turn & 1) == 1
        cos_raw = jnp.where(odd, sine, cosine)
        sin_raw = jnp.where(odd, cosine, sine)
        cos_sign = jnp.where(((turn + 1) & 2) == 2, -scale, scale)
        sin_sign = jnp.where((turn & 2) == 2, scale, -scale)
        cos_high, cos_low = split_pair(cos_raw * cos_sign)
        sin_high, sin_low = split_pair(sin_raw * sin_sign)
        for place, part in enumerate((cos_high, sin_high, cos_low, sin_low)):
            table_ref[place * freqs:(place + 1) * freqs, pl.ds(at, width)] = part
        return carry

    lax.fori_loop(0, steps // width, fill, 0)


def fill_stencils(ids_ref, weights_ref, ids_rows, high_rows, low_rows):
    ids = ids_ref[...]
    weights = weights_ref[...]
    count = ids.shape[0]
    merged = weights
    for shift in range(1, count):
        same = pltpu.roll(ids, shift, 0) == ids
        merged = merged + jnp.where(same, pltpu.roll(weights, shift, 0), 0.0)
    high, low = split_pair(merged)
    high = high.astype(F32)
    low = low.astype(F32)
    for k in range(count):
        rows = slice(16 * k, 16 * k + 16)
        full = (16, ids.shape[1])
        ids_rows[rows, :] = jnp.broadcast_to(ids[k:k + 1, :], full).astype(jnp.int16)
        high_rows[rows, :] = jnp.broadcast_to(high[k:k + 1, :], full).astype(BF16)
        low_rows[rows, :] = jnp.broadcast_to(low[k:k + 1, :], full).astype(BF16)


def fill_basis(base, points, ids_rows, high_rows, low_rows, basis_high, basis_low):
    count = ids_rows.shape[0] // 16
    group = 8
    for half in range(points // (16 * group)):
        rows_at = [half * 16 * group + 16 * g for g in range(group)]
        wanted = [
            (lax.broadcasted_iota(jnp.int32, (16, LANES), 0) + (base + at)).astype(jnp.int16) for at in rows_at
        ]
        for tile in range(ids_rows.shape[1] // LANES):
            lanes = slice(tile * LANES, (tile + 1) * LANES)
            high = [jnp.zeros((16, LANES), BF16)] * group
            low = [jnp.zeros((16, LANES), BF16)] * group
            for k in range(count):
                rows = slice(16 * k, 16 * k + 16)
                ids_k = ids_rows[rows, lanes]
                high_k = high_rows[rows, lanes]
                low_k = low_rows[rows, lanes]
                for g in range(group):
                    hit = wanted[g] == ids_k
                    high[g] = jnp.where(hit, high_k, high[g])
                    low[g] = jnp.where(hit, low_k, low[g])
            for g in range(group):
                basis_high[rows_at[g]:rows_at[g] + 16, lanes] = high[g]
                basis_low[rows_at[g]:rows_at[g] + 16, lanes] = low[g]


def fill_products(forces_ref, washes_ref, high_ref, low_ref):
    modes = forces_ref.shape[0]

    def fill(m, carry):
        at = pl.multiple_of(m * modes, modes)
        high, low = split_pair(forces_ref[pl.ds(m, 1), :] * washes_ref[...])
        high_ref[pl.ds(at, modes), :] = high
        low_ref[pl.ds(at, modes), :] = low
        return carry

    lax.fori_loop(0, modes, fill, 0)


def kernel(
    tm_count, panel_count,
    pressure_ref, freq_in, ids_in, weights_in, forces_in, washes_in,
    out_ref,
    freq_ref, ids_ref, weights_ref, forces_ref, washes_ref,
    pressure_buf, table, ids_rows, high_rows, low_rows, basis_high, basis_low,
    spectra_out, spectra_in, spectra_own, spectra_high, spectra_low,
    partial, first_buf, product_high, product_low, local, second_buf, gathered,
    small_sem, load_sem, swap_send, swap_recv, first_send, first_recv, second_send, second_recv,
    wide_send, wide_recv, core_send, core_recv, side_send, side_recv, last_send, last_recv,
):
    me_t = lax.axis_index("tm")
    me_p = lax.axis_index("panel")
    core = lax.rem(me_t, 2)
    side = me_t // 2
    sides = tm_count // 2

    def tm_at(rel):
        return 2 * lax.rem(side + rel // 2, sides) + lax.rem(core + rel % 2, 2)

    rels = range(1, tm_count)
    partner = tm_at(1)
    steps, points = pressure_ref.shape
    chunks = points // CHUNK
    cells = partial.shape[0]
    own_rows = cells // tm_count
    rows = local.shape[1]
    bands = own_rows // rows
    blocks = panel_count // bands

    own_chunks = chunks // 2

    def load(j):
        place = lax.rem(j + (1 - core) * own_chunks, chunks)
        return pltpu.make_async_copy(
            pressure_ref.at[:, pl.ds(pl.multiple_of(place * CHUNK, CHUNK), CHUNK)], pressure_buf.at[j], load_sem.at[j]
        )

    def swap(j):
        return pltpu.make_async_remote_copy(
            src_ref=spectra_out.at[j],
            dst_ref=spectra_in.at[j],
            send_sem=swap_send.at[j],
            recv_sem=swap_recv.at[j],
            device_id=(partner, me_p),
            device_id_type=MESH,
        )

    small = [
        pltpu.make_async_copy(source, target, small_sem.at[place])
        for place, (source, target) in enumerate((
            (freq_in, freq_ref), (ids_in, ids_ref), (weights_in, weights_ref),
            (forces_in, forces_ref), (washes_in, washes_ref),
        ))
    ]
    for copy in small:
        copy.start()
    for j in range(chunks):
        load(j).start()

    barrier = pltpu.get_barrier_semaphore()
    for rel in rels:
        pl.semaphore_signal(barrier, inc=1, device_id=(tm_at(rel), me_p), device_id_type=MESH)
    for d in range(1, panel_count):
        pl.semaphore_signal(
            barrier, inc=1, device_id=(me_t, lax.rem(me_p + d, panel_count)), device_id_type=MESH
        )

    small[0].wait()
    fill_table(freq_ref, table, me_t * steps, steps * tm_count)
    small[1].wait()
    small[2].wait()
    fill_stencils(ids_ref, weights_ref, ids_rows, high_rows, low_rows)

    def basis_step(j, carry):
        at = pl.multiple_of(j * LANES, LANES)
        fill_basis(
            core * own_chunks * CHUNK + at, LANES, ids_rows, high_rows, low_rows,
            basis_high.at[pl.ds(at, LANES)], basis_low.at[pl.ds(at, LANES)],
        )
        return carry

    lax.fori_loop(0, own_chunks * CHUNK // LANES, basis_step, 0)

    def transform(j):
        load(j).wait()
        block_high, block_low = split_pair(pressure_buf[j])
        wide = dot_rows(table[...], block_high)
        return wide[:cells] + wide[cells:] + dot_rows(table[:cells, :], block_low)

    pl.semaphore_wait(barrier, tm_count + panel_count - 2)

    def other_step(j, carry):
        spectra_out[j] = transform(j)
        swap(j).start()
        return carry

    def own_step(j, carry):
        spectra_own[j] = transform(own_chunks + j)
        return carry

    lax.fori_loop(0, own_chunks, other_step, 0)
    lax.fori_loop(0, own_chunks, own_step, 0)
    for j in range(own_chunks):
        swap(j).wait_recv()
        high, low = split_pair(spectra_own[j] + spectra_in[j])
        span = slice(j * CHUNK, (j + 1) * CHUNK)
        spectra_high[:, span] = high
        spectra_low[:, span] = low
    partial[...] = (
        dot_rows(spectra_high[...], basis_high[...])
        + dot_rows(spectra_low[...], basis_high[...])
        + dot_rows(spectra_high[...], basis_low[...])
    )

    first = {}
    for rel in reversed(rels):
        first[rel] = pltpu.make_async_remote_copy(
            src_ref=partial.at[pl.ds(pl.multiple_of(tm_at(rel) * own_rows, own_rows), own_rows)],
            dst_ref=first_buf.at[rel - 1],
            send_sem=first_send.at[rel - 1],
            recv_sem=first_recv.at[rel - 1],
            device_id=(tm_at(rel), me_p),
            device_id_type=MESH,
        )
        first[rel].start()
    small[3].wait()
    small[4].wait()
    fill_products(forces_ref, washes_ref, product_high, product_low)
    owned = partial[pl.ds(pl.multiple_of(me_t * own_rows, own_rows), own_rows), :]
    for rel in rels:
        first[rel].wait_recv()
        owned = owned + first_buf[rel - 1]
    owned_high, owned_low = split_pair(owned)
    for pair in range(blocks // 2):
        span = slice(pair * 2 * LANES, (pair + 1) * 2 * LANES)
        grams = (
            dot_lanes(owned_high, product_high[span, :])
            + dot_lanes(owned_low, product_high[span, :])
            + dot_lanes(owned_high, product_low[span, :])
        )
        for part in range(2):
            for band in range(bands):
                local[band * blocks + 2 * pair + part] = grams[
                    band * rows:(band + 1) * rows, part * LANES:(part + 1) * LANES
                ]

    second = []
    for d in range(1, panel_count):
        target = lax.rem(me_p + d, panel_count)
        copy = pltpu.make_async_remote_copy(
            src_ref=local.at[target],
            dst_ref=second_buf.at[d - 1],
            send_sem=second_send.at[d - 1],
            recv_sem=second_recv.at[d - 1],
            device_id=(me_t, target),
            device_id_type=MESH,
        )
        copy.start()
        second.append(copy)
    total = local[me_p]
    for d in range(1, panel_count):
        second[d - 1].wait_recv()
        total = total + second_buf[d - 1]
    gathered[me_t, me_p] = total

    def share(p, t, sends, recvs, index, device):
        place = gathered.at[t, p]
        copy = pltpu.make_async_remote_copy(
            src_ref=place,
            dst_ref=place,
            send_sem=sends.at[index],
            recv_sem=recvs.at[index],
            device_id=device,
            device_id_type=MESH,
        )
        return copy

    wide, to_core, to_side, last = [], [], [], []
    for d in range(1, panel_count):
        copy = share(me_p, me_t, wide_send, wide_recv, d - 1, (me_t, lax.rem(me_p + d, panel_count)))
        copy.start()
        wide.append(copy)
    for d in range(panel_count):
        origin = lax.rem(me_p + panel_count - d, panel_count)
        if d > 0:
            wide[d - 1].wait_recv()
        for hop in range(1, sides):
            copy = share(
                origin, me_t, side_send, side_recv, (hop - 1) * panel_count + d, (tm_at(2 * hop), me_p)
            )
            copy.start()
            to_side.append(copy)
        copy = share(origin, me_t, core_send, core_recv, d, (partner, me_p))
        copy.start()
        to_core.append(copy)
    for d in range(panel_count):
        origin = lax.rem(me_p + panel_count - d, panel_count)
        for hop in range(1, sides):
            to_side[d * (sides - 1) + hop - 1].wait_recv()
            copy = share(
                origin, tm_at(2 * (sides - hop)), last_send, last_recv, (hop - 1) * panel_count + d, (partner, me_p)
            )
            copy.start()
            last.append(copy)
    for copy in to_core + last:
        copy.wait_recv()

    def turn(block, carry):
        at = pl.multiple_of(block * LANES, LANES)
        for c in range(2):
            parts = [
                gathered[t, band * blocks + block]
                for t in range(c * sides, (c + 1) * sides)
                for band in range(bands)
            ]
            out_ref[c, pl.ds(at, LANES), :] = jnp.concatenate(parts, axis=0).T
        return carry

    lax.fori_loop(0, blocks, turn, 0)

    for j in range(own_chunks):
        swap(j).wait_send()
    for copy in list(first.values()) + second + wide + to_core + to_side + last:
        copy.wait_send()


def body(pressure, freq_bins, stencil_ids, spline_weights, mode_forces, mode_washes):
    tm_count = lax.axis_size("tm")
    panel_count = lax.axis_size("panel")
    steps, points = pressure.shape
    freqs = freq_bins.shape[0]
    panels, stencil = stencil_ids.shape
    modes = mode_forces.shape[0]
    cells = 2 * freqs
    own_rows = cells // tm_count
    blocks = modes * modes // LANES
    rows = own_rows * blocks // panel_count
    chunks = points // CHUNK
    vmem = pl.BlockSpec(memory_space=pltpu.VMEM)
    peers = panel_count - 1
    far = (tm_count // 2 - 1) * panel_count
    dma = pltpu.SemaphoreType.DMA
    grams = pl.pallas_call(
        functools.partial(kernel, tm_count, panel_count),
        out_shape=jax.ShapeDtypeStruct((2, modes * modes, freqs), F32),
        in_specs=[pl.BlockSpec(memory_space=pltpu.HBM)] * 6,
        out_specs=vmem,
        scratch_shapes=[
            pltpu.VMEM((1, freqs), jnp.int32),
            pltpu.VMEM((stencil, panels), jnp.int32),
            pltpu.VMEM((stencil, panels), F32),
            pltpu.VMEM((modes, panels), F32),
            pltpu.VMEM((modes, panels), F32),
            pltpu.VMEM((chunks, steps, CHUNK), F32),
            pltpu.VMEM((2 * cells, steps), BF16),
            pltpu.VMEM((16 * stencil, panels), jnp.int16),
            pltpu.VMEM((16 * stencil, panels), BF16),
            pltpu.VMEM((16 * stencil, panels), BF16),
            pltpu.VMEM((points // 2, panels), BF16),
            pltpu.VMEM((points // 2, panels), BF16),
            pltpu.VMEM((chunks // 2, cells, CHUNK), F32),
            pltpu.VMEM((chunks // 2, cells, CHUNK), F32),
            pltpu.VMEM((chunks // 2, cells, CHUNK), F32),
            pltpu.VMEM((cells, points // 2), BF16),
            pltpu.VMEM((cells, points // 2), BF16),
            pltpu.VMEM((cells, panels), F32),
            pltpu.VMEM((tm_count - 1, own_rows, panels), F32),
            pltpu.VMEM((modes * modes, panels), BF16),
            pltpu.VMEM((modes * modes, panels), BF16),
            pltpu.VMEM((panel_count, rows, LANES), F32),
            pltpu.VMEM((peers, rows, LANES), F32),
            pltpu.VMEM((tm_count, panel_count, rows, LANES), F32),
            dma((5,)),
            dma((chunks,)),
            dma((chunks // 2,)), dma((chunks // 2,)),
            dma((tm_count - 1,)), dma((tm_count - 1,)),
            dma((peers,)), dma((peers,)),
            dma((peers,)), dma((peers,)),
            dma((panel_count,)), dma((panel_count,)),
            dma((far,)), dma((far,)),
            dma((far,)), dma((far,)),
        ],
        compiler_params=pltpu.CompilerParams(
            collective_id=0, has_side_effects=True, vmem_limit_bytes=50 * 1024 * 1024
        ),
        cost_estimate=pl.CostEstimate(flops=4 * 10**9, bytes_accessed=10 * 2**20, transcendentals=0),
    )(
        *(
            pltpu.with_memory_space_constraint(array, pltpu.HBM)
            for array in (
                pressure, freq_bins.reshape(1, freqs), stencil_ids.T, spline_weights.T, mode_forces, mode_washes
            )
        )
    )
    return grams.reshape(2, modes, modes, freqs).transpose(0, 3, 1, 2)


def solution(mesh):
    placed = (
        P("tm", "panel"),
        P(),
        P("panel", None),
        P("panel", None),
        P(None, "panel"),
        P(None, "panel"),
    )
    return jax.shard_map(body, mesh=mesh, in_specs=placed, out_specs=P(), check_vma=False)
```

```python
import functools
import math

import jax
import jax.numpy as jnp
from jax import lax
from jax.experimental import pallas as pl
from jax.experimental.pallas import tpu as pltpu
from jax.sharding import PartitionSpec as P

F32 = jnp.float32
BF16 = jnp.bfloat16
LANES = 128
CHUNK = 512
MESH = pl.DeviceIdType.MESH


def split_pair(value):
    high = value.astype(BF16)
    return high, (value - high.astype(F32)).astype(BF16)


def dot_rows(left, right):
    return lax.dot_general(left, right, (((1,), (0,)), ((), ())), preferred_element_type=F32)


def dot_lanes(left, right):
    return lax.dot_general(left, right, (((1,), (1,)), ((), ())), preferred_element_type=F32)


def fill_table(freq_ref, table_ref, first, total):
    freqs = freq_ref.shape[1]
    steps = table_ref.shape[1]
    quarter = total // 4
    spread = jnp.broadcast_to(freq_ref[...].astype(F32), (freqs, freqs))
    on_diagonal = lax.broadcasted_iota(jnp.int32, (freqs, freqs), 0) == lax.broadcasted_iota(
        jnp.int32, (freqs, freqs), 1
    )
    column = jnp.sum(jnp.where(on_diagonal, spread, 0.0), axis=1, keepdims=True).astype(jnp.int32)
    scale = 1.0 / math.sqrt(total)
    width = 2 * LANES

    def fill(block, carry):
        at = pl.multiple_of(block * width, width)
        times = lax.broadcasted_iota(jnp.int32, (freqs, width), 1) + (first + at)
        phase = (column * times) & (total - 1)
        turn = (phase + quarter // 2) >> (quarter.bit_length() - 1)
        x = (phase - turn * quarter).astype(F32) * (2.0 * math.pi / total)
        z = x * x
        sine = x + x * z * (-1.6666654611e-1 + z * (8.3321608736e-3 + z * -1.9515295891e-4))
        cosine = 1.0 - 0.5 * z + z * z * (
            4.166664568298827e-2 + z * (-1.388731625493765e-3 + z * 2.443315711809948e-5)
        )
        odd = (turn & 1) == 1
        cos_raw = jnp.where(odd, sine, cosine)
        sin_raw = jnp.where(odd, cosine, sine)
        cos_sign = jnp.where(((turn + 1) & 2) == 2, -scale, scale)
        sin_sign = jnp.where((turn & 2) == 2, scale, -scale)
        cos_high, cos_low = split_pair(cos_raw * cos_sign)
        sin_high, sin_low = split_pair(sin_raw * sin_sign)
        for place, part in enumerate((cos_high, sin_high, cos_low, sin_low)):
            table_ref[place * freqs:(place + 1) * freqs, pl.ds(at, width)] = part
        return carry

    lax.fori_loop(0, steps // width, fill, 0)


def fill_stencils(ids_ref, weights_ref, ids_rows, high_rows, low_rows):
    ids = ids_ref[...]
    weights = weights_ref[...]
    count = ids.shape[0]
    merged = weights
    for shift in range(1, count):
        same = pltpu.roll(ids, shift, 0) == ids
        merged = merged + jnp.where(same, pltpu.roll(weights, shift, 0), 0.0)
    high, low = split_pair(merged)
    high = high.astype(F32)
    low = low.astype(F32)
    for k in range(count):
        rows = slice(16 * k, 16 * k + 16)
        full = (16, ids.shape[1])
        ids_rows[rows, :] = jnp.broadcast_to(ids[k:k + 1, :], full).astype(jnp.int16)
        high_rows[rows, :] = jnp.broadcast_to(high[k:k + 1, :], full).astype(BF16)
        low_rows[rows, :] = jnp.broadcast_to(low[k:k + 1, :], full).astype(BF16)


def fill_basis(base, points, ids_rows, high_rows, low_rows, basis_high, basis_low):
    count = ids_rows.shape[0] // 16
    group = 8
    for half in range(points // (16 * group)):
        rows_at = [half * 16 * group + 16 * g for g in range(group)]
        wanted = [
            (lax.broadcasted_iota(jnp.int32, (16, LANES), 0) + (base + at)).astype(jnp.int16) for at in rows_at
        ]
        for tile in range(ids_rows.shape[1] // LANES):
            lanes = slice(tile * LANES, (tile + 1) * LANES)
            high = [jnp.zeros((16, LANES), BF16)] * group
            low = [jnp.zeros((16, LANES), BF16)] * group
            for k in range(count):
                rows = slice(16 * k, 16 * k + 16)
                ids_k = ids_rows[rows, lanes]
                high_k = high_rows[rows, lanes]
                low_k = low_rows[rows, lanes]
                for g in range(group):
                    hit = wanted[g] == ids_k
                    high[g] = jnp.where(hit, high_k, high[g])
                    low[g] = jnp.where(hit, low_k, low[g])
            for g in range(group):
                basis_high[rows_at[g]:rows_at[g] + 16, lanes] = high[g]
                basis_low[rows_at[g]:rows_at[g] + 16, lanes] = low[g]


def fill_products(forces_ref, washes_ref, high_ref, low_ref):
    modes = forces_ref.shape[0]

    def fill(m, carry):
        at = pl.multiple_of(m * modes, modes)
        high, low = split_pair(forces_ref[pl.ds(m, 1), :] * washes_ref[...])
        high_ref[pl.ds(at, modes), :] = high
        low_ref[pl.ds(at, modes), :] = low
        return carry

    lax.fori_loop(0, modes, fill, 0)


def kernel(
    tm_count, panel_count,
    pressure_ref, freq_in, ids_in, weights_in, forces_in, washes_in,
    out_ref,
    freq_ref, ids_ref, weights_ref, forces_ref, washes_ref,
    pressure_buf, table, ids_rows, high_rows, low_rows, basis_high, basis_low,
    spectra_out, spectra_in, spectra_own, spectra_high, spectra_low,
    partial, first_buf, product_high, product_low, local, second_buf, gathered,
    small_sem, load_sem, swap_send, swap_recv, first_send, first_recv, second_send, second_recv,
    wide_send, wide_recv, core_send, core_recv, side_send, side_recv, last_send, last_recv,
):
    me_t = lax.axis_index("tm")
    me_p = lax.axis_index("panel")
    core = lax.rem(me_t, 2)
    side = me_t // 2
    sides = tm_count // 2

    def tm_at(rel):
        return 2 * lax.rem(side + rel // 2, sides) + lax.rem(core + rel % 2, 2)

    rels = range(1, tm_count)
    partner = tm_at(1)
    steps, points = pressure_ref.shape
    chunks = points // CHUNK
    cells = partial.shape[0]
    own_rows = cells // tm_count
    rows = local.shape[1]
    bands = own_rows // rows
    blocks = panel_count // bands

    own_chunks = chunks // 2

    def load(j):
        place = lax.rem(j + (1 - core) * own_chunks, chunks)
        return pltpu.make_async_copy(
            pressure_ref.at[:, pl.ds(pl.multiple_of(place * CHUNK, CHUNK), CHUNK)], pressure_buf.at[j], load_sem.at[j]
        )

    def swap(j):
        return pltpu.make_async_remote_copy(
            src_ref=spectra_out.at[j],
            dst_ref=spectra_in.at[j],
            send_sem=swap_send.at[j],
            recv_sem=swap_recv.at[j],
            device_id=(partner, me_p),
            device_id_type=MESH,
        )

    small = [
        pltpu.make_async_copy(source, target, small_sem.at[place])
        for place, (source, target) in enumerate((
            (freq_in, freq_ref), (ids_in, ids_ref), (weights_in, weights_ref),
            (forces_in, forces_ref), (washes_in, washes_ref),
        ))
    ]
    for copy in small:
        copy.start()
    for j in range(chunks):
        load(j).start()

    barrier = pltpu.get_barrier_semaphore()
    for rel in rels:
        pl.semaphore_signal(barrier, inc=1, device_id=(tm_at(rel), me_p), device_id_type=MESH)
    for d in range(1, panel_count):
        pl.semaphore_signal(
            barrier, inc=1, device_id=(me_t, lax.rem(me_p + d, panel_count)), device_id_type=MESH
        )

    small[0].wait()
    fill_table(freq_ref, table, me_t * steps, steps * tm_count)
    small[1].wait()
    small[2].wait()
    fill_stencils(ids_ref, weights_ref, ids_rows, high_rows, low_rows)

    def basis_step(j, carry):
        at = pl.multiple_of(j * LANES, LANES)
        fill_basis(
            core * own_chunks * CHUNK + at, LANES, ids_rows, high_rows, low_rows,
            basis_high.at[pl.ds(at, LANES)], basis_low.at[pl.ds(at, LANES)],
        )
        return carry

    lax.fori_loop(0, own_chunks * CHUNK // LANES, basis_step, 0)

    def transform(j):
        load(j).wait()
        block_high, block_low = split_pair(pressure_buf[j])
        wide = dot_rows(table[...], block_high)
        return wide[:cells] + wide[cells:] + dot_rows(table[:cells, :], block_low)

    pl.semaphore_wait(barrier, tm_count + panel_count - 2)

    def other_step(j, carry):
        spectra_out[j] = transform(j)
        swap(j).start()
        return carry

    def own_step(j, carry):
        spectra_own[j] = transform(own_chunks + j)
        return carry

    lax.fori_loop(0, own_chunks, other_step, 0)
    lax.fori_loop(0, own_chunks, own_step, 0)
    for j in range(own_chunks):
        swap(j).wait_recv()
        high, low = split_pair(spectra_own[j] + spectra_in[j])
        span = slice(j * CHUNK, (j + 1) * CHUNK)
        spectra_high[:, span] = high
        spectra_low[:, span] = low
    partial[...] = (
        dot_rows(spectra_high[...], basis_high[...])
        + dot_rows(spectra_low[...], basis_high[...])
        + dot_rows(spectra_high[...], basis_low[...])
    )

    first = {}
    for rel in reversed(rels):
        first[rel] = pltpu.make_async_remote_copy(
            src_ref=partial.at[pl.ds(pl.multiple_of(tm_at(rel) * own_rows, own_rows), own_rows)],
            dst_ref=first_buf.at[rel - 1],
            send_sem=first_send.at[rel - 1],
            recv_sem=first_recv.at[rel - 1],
            device_id=(tm_at(rel), me_p),
            device_id_type=MESH,
        )
        first[rel].start()
    small[3].wait()
    small[4].wait()
    fill_products(forces_ref, washes_ref, product_high, product_low)
    owned = partial[pl.ds(pl.multiple_of(me_t * own_rows, own_rows), own_rows), :]
    for rel in rels:
        first[rel].wait_recv()
        owned = owned + first_buf[rel - 1]
    owned_high, owned_low = split_pair(owned)
    for pair in range(blocks // 2):
        span = slice(pair * 2 * LANES, (pair + 1) * 2 * LANES)
        grams = (
            dot_lanes(owned_high, product_high[span, :])
            + dot_lanes(owned_low, product_high[span, :])
            + dot_lanes(owned_high, product_low[span, :])
        )
        for part in range(2):
            for band in range(bands):
                local[band * blocks + 2 * pair + part] = grams[
                    band * rows:(band + 1) * rows, part * LANES:(part + 1) * LANES
                ]

    owners = panel_count // 2
    lowest = panel_count // 4
    mine = me_p - lowest
    is_owner = jnp.logical_and(mine >= 0, mine < owners)
    base = jnp.minimum(jnp.maximum(mine, 0), owners - 1)

    def reduce_to(q, slot):
        return pltpu.make_async_remote_copy(
            src_ref=local.at[pl.ds(2 * q, 2)],
            dst_ref=second_buf.at[slot],
            send_sem=second_send.at[q],
            recv_sem=second_recv.at[slot],
            device_id=(me_t, lowest + q),
            device_id_type=MESH,
        )

    def share(q, t, send, recv, device):
        place = gathered.at[t, pl.ds(2 * q, 2)]
        return pltpu.make_async_remote_copy(
            src_ref=place, dst_ref=place, send_sem=send, recv_sem=recv, device_id=device, device_id_type=MESH
        )

    def spread(p):
        return share(base, me_t, wide_send.at[p], wide_recv.at[base], (me_t, p))

    for q in range(owners):
        @pl.when(me_p != lowest + q)
        def _():
            reduce_to(q, me_p).start()

    @pl.when(is_owner)
    def _():
        total = local[pl.ds(2 * base, 2)]
        second_buf[me_p] = total
        for p in range(panel_count):
            @pl.when(me_p != p)
            def _():
                reduce_to(base, p).wait_recv()
        total = second_buf[0]
        for p in range(1, panel_count):
            total = total + second_buf[p]
        gathered[me_t, pl.ds(2 * base, 2)] = total
        for p in range(panel_count):
            @pl.when(me_p != p)
            def _():
                spread(p).start()

    to_core, to_side, last = [], [], []
    for step in range(owners):
        q = lax.rem(base + step, owners)

        @pl.when(me_p != lowest + q)
        def _():
            share(q, me_t, wide_send.at[me_p], wide_recv.at[q], (me_t, lowest + q)).wait_recv()

        for hop in range(1, sides):
            at = (hop - 1) * owners + step
            copy = share(q, me_t, side_send.at[at], side_recv.at[at], (tm_at(2 * hop), me_p))
            copy.start()
            to_side.append(copy)
        copy = share(q, me_t, core_send.at[step], core_recv.at[step], (partner, me_p))
        copy.start()
        to_core.append(copy)
    for step in range(owners):
        q = lax.rem(base + step, owners)
        for hop in range(1, sides):
            at = (hop - 1) * owners + step
            to_side[step * (sides - 1) + hop - 1].wait_recv()
            copy = share(
                q, tm_at(2 * (sides - hop)), last_send.at[at], last_recv.at[at], (partner, me_p)
            )
            copy.start()
            last.append(copy)
    for copy in to_core + last:
        copy.wait_recv()

    def turn(block, carry):
        at = pl.multiple_of(block * LANES, LANES)
        for c in range(2):
            parts = [
                gathered[t, band * blocks + block]
                for t in range(c * sides, (c + 1) * sides)
                for band in range(bands)
            ]
            out_ref[c, pl.ds(at, LANES), :] = jnp.concatenate(parts, axis=0).T
        return carry

    lax.fori_loop(0, blocks, turn, 0)

    for j in range(own_chunks):
        swap(j).wait_send()
    for copy in list(first.values()) + to_core + to_side + last:
        copy.wait_send()
    for q in range(owners):
        @pl.when(me_p != lowest + q)
        def _():
            reduce_to(q, me_p).wait_send()

    @pl.when(is_owner)
    def _():
        for p in range(panel_count):
            @pl.when(me_p != p)
            def _():
                spread(p).wait_send()


def body(pressure, freq_bins, stencil_ids, spline_weights, mode_forces, mode_washes):
    tm_count = lax.axis_size("tm")
    panel_count = lax.axis_size("panel")
    steps, points = pressure.shape
    freqs = freq_bins.shape[0]
    panels, stencil = stencil_ids.shape
    modes = mode_forces.shape[0]
    cells = 2 * freqs
    own_rows = cells // tm_count
    blocks = modes * modes // LANES
    rows = own_rows * blocks // panel_count
    chunks = points // CHUNK
    vmem = pl.BlockSpec(memory_space=pltpu.VMEM)
    owners = panel_count // 2
    far = (tm_count // 2 - 1) * owners
    dma = pltpu.SemaphoreType.DMA
    grams = pl.pallas_call(
        functools.partial(kernel, tm_count, panel_count),
        out_shape=jax.ShapeDtypeStruct((2, modes * modes, freqs), F32),
        in_specs=[pl.BlockSpec(memory_space=pltpu.HBM)] * 6,
        out_specs=vmem,
        scratch_shapes=[
            pltpu.VMEM((1, freqs), jnp.int32),
            pltpu.VMEM((stencil, panels), jnp.int32),
            pltpu.VMEM((stencil, panels), F32),
            pltpu.VMEM((modes, panels), F32),
            pltpu.VMEM((modes, panels), F32),
            pltpu.VMEM((chunks, steps, CHUNK), F32),
            pltpu.VMEM((2 * cells, steps), BF16),
            pltpu.VMEM((16 * stencil, panels), jnp.int16),
            pltpu.VMEM((16 * stencil, panels), BF16),
            pltpu.VMEM((16 * stencil, panels), BF16),
            pltpu.VMEM((points // 2, panels), BF16),
            pltpu.VMEM((points // 2, panels), BF16),
            pltpu.VMEM((chunks // 2, cells, CHUNK), F32),
            pltpu.VMEM((chunks // 2, cells, CHUNK), F32),
            pltpu.VMEM((chunks // 2, cells, CHUNK), F32),
            pltpu.VMEM((cells, points // 2), BF16),
            pltpu.VMEM((cells, points // 2), BF16),
            pltpu.VMEM((cells, panels), F32),
            pltpu.VMEM((tm_count - 1, own_rows, panels), F32),
            pltpu.VMEM((modes * modes, panels), BF16),
            pltpu.VMEM((modes * modes, panels), BF16),
            pltpu.VMEM((panel_count, rows, LANES), F32),
            pltpu.VMEM((panel_count, 2, rows, LANES), F32),
            pltpu.VMEM((tm_count, panel_count, rows, LANES), F32),
            dma((5,)),
            dma((chunks,)),
            dma((chunks // 2,)), dma((chunks // 2,)),
            dma((tm_count - 1,)), dma((tm_count - 1,)),
            dma((owners,)), dma((panel_count,)),
            dma((panel_count,)), dma((owners,)),
            dma((owners,)), dma((owners,)),
            dma((far,)), dma((far,)),
            dma((far,)), dma((far,)),
        ],
        compiler_params=pltpu.CompilerParams(
            collective_id=0, has_side_effects=True, vmem_limit_bytes=50 * 1024 * 1024
        ),
        cost_estimate=pl.CostEstimate(flops=4 * 10**9, bytes_accessed=10 * 2**20, transcendentals=0),
    )(
        *(
            pltpu.with_memory_space_constraint(array, pltpu.HBM)
            for array in (
                pressure, freq_bins.reshape(1, freqs), stencil_ids.T, spline_weights.T, mode_forces, mode_washes
            )
        )
    )
    return grams.reshape(2, modes, modes, freqs).transpose(0, 3, 1, 2)


def solution(mesh):
    placed = (
        P("tm", "panel"),
        P(),
        P("panel", None),
        P("panel", None),
        P(None, "panel"),
        P(None, "panel"),
    )
    return jax.shard_map(body, mesh=mesh, in_specs=placed, out_specs=P(), check_vma=False)
```
